256 devices in a mesh: row: 8 (over z), col: 16 (over y, x), dp: 2 (over core).
Axes of the slice: x: 4, y: 4, z: 8, core: 2. Of those that a mesh axis runs over, the one named last changes fastest.
Arguments:
- tokens: bfloat16 [2048, 6144], P(('col', 'dp'), 'row'), may hold values from -6 to 6
- in_weight: bfloat16 [6144, 24576], P('row', 'col'), may hold values from -0.078125 to 0.078125
- out_weight: bfloat16 [24576, 6144], P('col', 'row'), may hold values from -0.0390625 to 0.0390625
- output_grad: bfloat16 [2048, 6144], P(('col', 'dp'), 'row'), may hold values from -6 to 6
Outputs:
- output: bfloat16 [2048, 6144], P(('col', 'dp'), 'row')
- input_grad: bfloat16 [2048, 6144], P(('col', 'dp'), 'row')
- in_weight_grad: bfloat16 [6144, 24576], P('row', ('col', 'dp'))
- out_weight_grad: bfloat16 [24576, 6144], P('col', ('row', 'dp'))
The draws below stay inside these ranges and needn't reach their ends.
All inputs are finite; a program needn't handle non-finite values.
Results may differ from the reference program's by a relative error of at most 0.0049.
Values may be sent and summed in bfloat16 or wider, within the bound.
No kernel may reach another device: no remote copies, remote signals or barrier semaphores. Data moves between devices by JAX's collectives and lax.ppermute only.
A program may use at most 128 MiB of HBM per device.

```python
import jax
import jax.numpy as jnp
from jax import lax

D = 6144
FF = 24576
TOKENS = 2048


def steps_of(rng, shape, cuts, low, top_value):
    factor_of = 1.0
    for position, blocks in cuts:
        draws = jax.random.uniform(jax.random.fold_in(jax.random.fold_in(rng, 6), position), (blocks,), jnp.float32, low / len(cuts), top_value / len(cuts))
        factor_of = factor_of * jnp.repeat(jnp.exp(draws), shape[position] // blocks).reshape((-1,) + (1,) * (len(shape) - 1 - position))
    return factor_of


def centred(rng, extent, spread, limit, shards=(), dtype=jnp.bfloat16):
    result = jax.random.normal(rng, extent, jnp.float32) * spread
    if len(shards) > 0:
        result = steps_of(rng, extent, shards, -0.22, 0.18) * result
    return jnp.clip(result, min=-limit, max=limit).astype(dtype)


def setup_inputs(seed: int = 0) -> dict:
    seeds = jax.random.split(jax.random.key(seed), 5)
    return {
        "tokens": centred(seeds[0], (TOKENS, D), 1.0, 6.0, ((0, 32), (1, 8))),
        "in_weight": centred(seeds[1], (D, FF), D ** -0.5, 0.078125, ((0, 8), (1, 16))),
        "out_weight": centred(seeds[2], (FF, D), FF ** -0.5, 0.0390625, ((0, 16), (1, 8))),
        "output_grad": centred(seeds[3], (TOKENS, D), 1.0, 6.0, ((0, 32), (1, 8))),
    }


root_half = 0.7071067811865476
inv_root_tau = 0.3989422804014327


def gelu_value(value):
    return value * 0.5 * (1.0 + lax.erf(value * root_half))


def gelu_slope(value):
    normal_cdf = 0.5 * (1.0 + lax.erf(value * root_half))
    return normal_cdf + value * jnp.exp(-0.5 * value * value) * inv_root_tau


def reference(tokens, in_weight, out_weight, output_grad):
    preact = jnp.dot(tokens, in_weight, preferred_element_type=jnp.float32)
    hidden = gelu_value(preact).astype(jnp.bfloat16)
    output = jnp.dot(hidden, out_weight, preferred_element_type=jnp.float32).astype(jnp.bfloat16)
    hidden_grad = jnp.dot(output_grad, out_weight.T, preferred_element_type=jnp.float32)
    preact_grad = (hidden_grad * gelu_slope(preact)).astype(jnp.bfloat16)
    input_grad = jnp.dot(preact_grad, in_weight.T, preferred_element_type=jnp.float32).astype(jnp.bfloat16)
    in_weight_grad = jnp.dot(tokens.T, preact_grad, preferred_element_type=jnp.float32).astype(jnp.bfloat16)
    out_weight_grad = jnp.dot(hidden.T, output_grad, preferred_element_type=jnp.float32).astype(jnp.bfloat16)
    return (output, input_grad, in_weight_grad, out_weight_grad)
```

```python
import jax
import jax.numpy as jnp
from jax import lax
from jax.sharding import PartitionSpec as P

root_half = 0.7071067811865476
inv_root_tau = 0.3989422804014327
f32, bf16 = jnp.float32, jnp.bfloat16


def gelu_value(value):
    return value * 0.5 * (1.0 + lax.erf(value * root_half))


def gelu_slope(value):
    normal_cdf = 0.5 * (1.0 + lax.erf(value * root_half))
    return normal_cdf + value * jnp.exp(-0.5 * value * value) * inv_root_tau


def dot(left, right, left_dim=1, right_dim=0):
    return lax.dot_general(
        left, right, (((left_dim,), (right_dim,)), ((), ())), preferred_element_type=f32
    )


def shift_z(value, step):
    return lax.ppermute(value, "row", [(i, (i + step) % 8) for i in range(8)])


def shift_x(value, step):
    pairs = [(y * 4 + x, y * 4 + (x + step) % 4) for y in range(4) for x in range(4)]
    return lax.ppermute(value, "col", pairs)


def shift_y(value, step):
    pairs = [(y * 4 + x, (y + step) % 4 * 4 + x) for y in range(4) for x in range(4)]
    return lax.ppermute(value, "col", pairs)


def swap_dp(value):
    return lax.ppermute(value, "dp", [(0, 1), (1, 0)])


def gather_plane(block):
    line = jnp.concatenate(
        [block, shift_x(block, -1), shift_x(block, 2), shift_x(block, 1)], axis=0
    )
    up, down = shift_y(line, -1), shift_y(line, 1)
    half = line.shape[0] // 2
    across = [shift_y(up[:half], -1), shift_y(down[half:], 1)]
    return jnp.concatenate([line, up] + across + [down], axis=0)


def scatter_plane(partial):
    rows, half = partial.shape[0] // 4, partial.shape[1] // 2
    own, up, far, down = (partial[i * rows : (i + 1) * rows] for i in range(4))
    from_down = shift_y(far[:, :half].astype(bf16), 1).astype(f32)
    from_up = shift_y(far[:, half:].astype(bf16), -1).astype(f32)
    up = jnp.concatenate([up[:, :half] + from_down, up[:, half:]], axis=1)
    down = jnp.concatenate([down[:, :half], down[:, half:] + from_up], axis=1)
    line = own + shift_y(up.astype(bf16), 1).astype(f32) + shift_y(down.astype(bf16), -1).astype(f32)
    rows = rows // 4
    own, right, far, left = (line[i * rows : (i + 1) * rows] for i in range(4))
    return (
        own
        + shift_x(right.astype(bf16), 1).astype(f32)
        + shift_x(far.astype(bf16), 2).astype(f32)
        + shift_x(left.astype(bf16), -1).astype(f32)
    )


def scatter_z(part):
    far = part(4)
    half = far.shape[1] // 2
    ahead = shift_z(far[:, :half].astype(bf16), 1).astype(f32)
    behind = shift_z(far[:, half:].astype(bf16), -1).astype(f32)
    three, five = part(3), part(5)
    ahead = jnp.concatenate([three[:, :half] + ahead, three[:, half:]], axis=1)
    behind = jnp.concatenate([five[:, :half], five[:, half:] + behind], axis=1)
    for k in (2, 1, 0):
        ahead = shift_z(ahead.astype(bf16), 1).astype(f32)
        behind = shift_z(behind.astype(bf16), -1).astype(f32)
        if k:
            ahead, behind = part(k) + ahead, part(8 - k) + behind
    return part(0) + ahead + behind


def gather_z(block):
    rows = block.shape[0] // 2
    found = {0: block}
    low = high = block
    for k in (1, 2, 3):
        low, high = shift_z(low, 1), shift_z(high, -1)
        found[8 - k], found[k] = low, high
    found[4] = jnp.concatenate([shift_z(high[:rows], -1), shift_z(low[rows:], 1)], axis=0)
    return [found[k] for k in range(8)]


def turned(value, place):
    return lax.dynamic_slice_in_dim(
        jnp.concatenate([value, value], axis=0), place, value.shape[0], axis=0
    )


def shards(tokens, in_weight, out_weight, output_grad):
    z, dp = lax.axis_index("row"), lax.axis_index("dp")
    tokens_all = gather_plane(tokens)
    grad_all = gather_plane(output_grad)
    tokens_turned = turned(tokens_all, z * 128)
    grad_turned = turned(grad_all, z * 128)

    preact = scatter_z(lambda k: dot(tokens_turned[128 * k : 128 * k + 128], in_weight))
    hidden_grad = scatter_z(lambda k: dot(grad_turned[128 * k : 128 * k + 128], out_weight, 1, 1))
    hidden = gelu_value(preact).astype(bf16)
    back = (8 - z) % 8 * 128
    hidden_all = turned(jnp.concatenate(gather_z(hidden), axis=0), back)
    output = scatter_plane(dot(hidden_all, out_weight))

    first = dp == 0
    width = grad_all.shape[1] // 2
    grad_kept = jnp.where(first, grad_all[:, :width], grad_all[:, width:])
    grad_sent = jnp.where(first, grad_all[:, width:], grad_all[:, :width])
    second_sum = swap_dp(dot(hidden_all, grad_sent, 0, 0)) + dot(hidden_all, grad_kept, 0, 0)

    preact_grad = (hidden_grad * gelu_slope(preact)).astype(bf16)
    preact_grad_all = turned(jnp.concatenate(gather_z(preact_grad), axis=0), back)
    input_grad = scatter_plane(dot(preact_grad_all, in_weight, 1, 1))
    width = preact_grad_all.shape[1] // 2
    kept = jnp.where(first, preact_grad_all[:, :width], preact_grad_all[:, width:])
    sent = jnp.where(first, preact_grad_all[:, width:], preact_grad_all[:, :width])
    first_sum = swap_dp(dot(tokens_all, sent, 0, 0)) + dot(tokens_all, kept, 0, 0)
    return (
        output.astype(bf16),
        input_grad.astype(bf16),
        first_sum.astype(bf16),
        second_sum.astype(bf16),
    )


def solution(mesh):
    in_specs = (P(("col", "dp"), "row"), P("row", "col"), P("col", "row"), P(("col", "dp"), "row"))
    out_specs = (
        P(("col", "dp"), "row"),
        P(("col", "dp"), "row"),
        P("row", ("col", "dp")),
        P("col", ("row", "dp")),
    )
    return jax.shard_map(shards, mesh=mesh, in_specs=in_specs, out_specs=out_specs, check_vma=False)
```

```python
import jax
import jax.numpy as jnp
from jax import lax
from jax.experimental import pallas as pl
from jax.experimental.pallas import tpu as pltpu
from jax.sharding import PartitionSpec as P

root_half = 0.7071067811865476
inv_root_tau = 0.3989422804014327
f32, bf16 = jnp.float32, jnp.bfloat16


def gelu_value(value):
    return value * 0.5 * (1.0 + lax.erf(value * root_half))


def gelu_slope(value):
    normal_cdf = 0.5 * (1.0 + lax.erf(value * root_half))
    return normal_cdf + value * jnp.exp(-0.5 * value * value) * inv_root_tau


def dot(left, right, left_dim=1, right_dim=0):
    return lax.dot_general(
        left, right, (((left_dim,), (right_dim,)), ((), ())), preferred_element_type=f32
    )


def shift_z(value, step):
    return lax.ppermute(value, "row", [(i, (i + step) % 8) for i in range(8)])


def shift_x(value, step):
    pairs = [(y * 4 + x, y * 4 + (x + step) % 4) for y in range(4) for x in range(4)]
    return lax.ppermute(value, "col", pairs)


def shift_y(value, step):
    pairs = [(y * 4 + x, (y + step) % 4 * 4 + x) for y in range(4) for x in range(4)]
    return lax.ppermute(value, "col", pairs)


def swap_dp(value):
    return lax.ppermute(value, "dp", [(0, 1), (1, 0)])


def gate(*arrays):
    def kernel(*refs):
        pass

    return pl.pallas_call(
        kernel,
        out_shape=[jax.ShapeDtypeStruct(array.shape, array.dtype) for array in arrays],
        in_specs=[pl.BlockSpec(memory_space=pl.ANY)] * len(arrays),
        out_specs=[pl.BlockSpec(memory_space=pl.ANY)] * len(arrays),
        input_output_aliases={i: i for i in range(len(arrays))},
        compiler_params=pltpu.CompilerParams(vmem_limit_bytes=2**18),
        name="gate",
    )(*arrays)


def lay(groups, place=None, after=()):
    shift = jnp.zeros((1,), jnp.int32) if place is None else place.astype(jnp.int32).reshape(1)
    arrays = [part for parts, _ in groups for _, part in parts]
    rows = [sum(part.shape[0] for _, part in parts) for parts, _ in groups]
    width = arrays[0].shape[1]

    def kernel(shift_ref, *refs):
        sources, outs, sems = refs[: len(arrays)], refs[-1 - len(groups) : -1], refs[-1]
        copies = []
        at = 0
        for (parts, spread), out in zip(groups, outs):
            for first, part in parts:
                if place is not None:
                    first = lax.rem(shift_ref[0] * 128 + first, out.shape[0])
                    first = pl.multiple_of(first, 64)
                size = part.shape[0] if spread == 64 else 64
                for row in range(0, part.shape[0], size):
                    target = out.at[pl.ds(first + row // 64 * spread, size)]
                    source = sources[at].at[pl.ds(row, size)]
                    copies.append(pltpu.make_async_copy(source, target, sems.at[len(copies)]))
                at += 1
        for copy in copies:
            copy.start()
        for copy in copies:
            copy.wait()

    size = sum(rows) * width * arrays[0].dtype.itemsize
    return pl.pallas_call(
        kernel,
        out_shape=[jax.ShapeDtypeStruct((count, width), arrays[0].dtype) for count in rows],
        in_specs=[pl.BlockSpec(memory_space=pltpu.SMEM)]
        + [pl.BlockSpec(memory_space=pl.ANY)] * (len(arrays) + len(after)),
        out_specs=[pl.BlockSpec(memory_space=pltpu.VMEM)] * len(groups),
        scratch_shapes=[pltpu.SemaphoreType.DMA((sum(rows) // 64,))],
        cost_estimate=pl.CostEstimate(flops=0, bytes_accessed=2 * size, transcendentals=0),
        compiler_params=pltpu.CompilerParams(vmem_limit_bytes=size + 2**20),
        name="lay",
    )(shift, *arrays, *after)


def send_line(block):
    return [(0, block), (64, shift_x(block, -1)), (128, shift_x(block, 2)), (192, shift_x(block, 1))]


def lay_plane(line, up, down, across):
    return lay([([(0, line), (256, up), (512, across[0]), (640, across[1]), (768, down)], 64)])[0]


def ring_terms(partial, first):
    width = partial.shape[1]
    if first is shift_x:
        return [partial.reshape(4, 4, 64, width)[:, i].reshape(256, width) for i in range(4)]
    return [partial[256 * i : 256 * i + 256] for i in range(4)]


def far_terms(terms):
    half = terms[2].shape[1] // 2
    return terms[2][:, :half], terms[2][:, half:]


def near_terms(terms, from_down, from_up):
    half = terms[2].shape[1] // 2
    up = jnp.concatenate([terms[1][:, :half] + from_down, terms[1][:, half:]], axis=1)
    down = jnp.concatenate([terms[3][:, :half], terms[3][:, half:] + from_up], axis=1)
    return up.astype(bf16), down.astype(bf16)


def line_terms(terms, from_down, from_up):
    line = terms[0] + from_down.astype(f32) + from_up.astype(f32)
    return [line[64 * i : 64 * i + 64] for i in range(4)]


def send_straight(parts, way):
    return way(parts[0], 1), way(parts[1], 2), way(parts[2], -1)


def both(ahead, behind, way=shift_z):
    return way(ahead, 1), way(behind, -1)


def shards(tokens, in_weight, out_weight, output_grad):
    z, dp = lax.axis_index("row"), lax.axis_index("dp")

    def halves(value):
        width = value.shape[1] // 2
        left, right = value[:, :width], value[:, width:]
        return jnp.where(dp == 0, left, right), jnp.where(dp == 0, right, left)

    def term(value, weight, weight_dim):
        def of(k):
            block = lax.dynamic_slice_in_dim(value, (z + k) % 8 * 128, 128, axis=0)
            return dot(block, weight, 1, weight_dim)

        return of

    def far_of(of):
        far = of(4).astype(bf16)
        return far[:, :768], far[:, 768:]

    def next_of(of, k, ahead, behind):
        if k == 3:
            three, five = of(3), of(5)
            ahead = jnp.concatenate([three[:, :768] + ahead.astype(f32), three[:, 768:]], axis=1)
            behind = jnp.concatenate([five[:, :768], five[:, 768:] + behind.astype(f32)], axis=1)
        else:
            ahead, behind = of(k) + ahead.astype(f32), of(8 - k) + behind.astype(f32)
        return ahead.astype(bf16), behind.astype(bf16)

    (line,) = lay([(send_line(tokens), 64)])
    line, late = gate(line, output_grad)
    sides = shift_y(line, -1), shift_y(line, 1)
    (grad_line,) = lay([(send_line(late), 64)])
    up, down, grad_line = gate(*sides, grad_line)
    across = shift_y(up[:128], -1), shift_y(down[128:], 1)
    sides = shift_y(grad_line, -1), shift_y(grad_line, 1)
    tokens_all = lay_plane(line, up, down, across)
    preact_of = term(tokens_all, in_weight, 0)
    ahead, behind, grad_up, grad_down = gate(*far_of(preact_of), *sides)

    across = shift_y(grad_up[:128], -1), shift_y(grad_down[128:], 1)
    ahead, behind = both(ahead, behind)
    grad_all = lay_plane(grad_line, grad_up, grad_down, across)
    grad_of = term(grad_all, out_weight, 1)
    ahead, behind, grad_all = gate(*next_of(preact_of, 3, ahead, behind), grad_all)
    ahead, behind = both(ahead, behind)
    ahead, behind, low, high = gate(*next_of(preact_of, 2, ahead, behind), *far_of(grad_of))
    ahead, behind = both(ahead, behind)
    low, high = both(low, high)
    ahead, behind, low, high = gate(
        *next_of(preact_of, 1, ahead, behind), *next_of(grad_of, 3, low, high)
    )
    ahead, behind = both(ahead, behind)
    low, high = both(low, high)
    preact = preact_of(0) + ahead.astype(f32) + behind.astype(f32)
    hidden = gelu_value(preact).astype(bf16)
    slope = gelu_slope(preact)
    hidden, low, high = gate(hidden, *next_of(grad_of, 2, low, high))
    found = [(0, hidden)]
    ahead, behind = both(hidden, hidden)
    low, high = both(low, high)
    ahead, behind, low, high = gate(ahead, behind, *next_of(grad_of, 1, low, high))
    found += [(896, ahead), (128, behind)]
    ahead, behind = both(ahead, behind)
    low, high = both(low, high)
    hidden_grad = grad_of(0) + low.astype(f32) + high.astype(f32)
    preact_grad = (hidden_grad * slope).astype(bf16)
    ahead, behind, preact_grad = gate(ahead, behind, preact_grad)
    found += [(768, ahead), (256, behind)]
    found_grad = [(0, preact_grad)]
    ahead, behind = both(ahead, behind)
    low, high = both(preact_grad, preact_grad)
    ahead, behind, low, high = gate(ahead, behind, low, high)
    found += [(640, ahead), (384, behind)]
    found_grad += [(896, low), (128, high)]
    ahead, behind = both(ahead[64:], behind[:64])
    low, high = both(low, high)
    ahead, behind, low, high = gate(ahead, behind, low, high)
    found += [(576, ahead), (512, behind)]
    found_grad += [(768, low), (256, high)]
    low, high = both(low, high)
    (hidden_all,) = lay([(found, 64)], z)
    out_terms = ring_terms(dot(hidden_all, out_weight), shift_x)
    low, high, far, far_up, hidden_all = gate(low, high, *far_terms(out_terms), hidden_all)
    found_grad += [(640, low), (384, high)]
    low, high = both(low[64:], high[:64])
    from_down, from_up = both(far, far_up, shift_x)
    kept, sent = halves(grad_all)
    second_sent = dot(hidden_all, sent, 0, 0)
    found_grad += [(576, low), (512, high)]

    (preact_grad_all,) = lay([(found_grad, 64)], z)
    in_terms = ring_terms(dot(preact_grad_all, in_weight, 1, 1), shift_y)
    far, far_up, up, down, preact_grad_all, second_sent = gate(
        *far_terms(in_terms), *near_terms(out_terms, from_down, from_up), preact_grad_all, second_sent
    )
    low, high = both(far, far_up, shift_y)
    from_down, from_up = both(up, down, shift_x)
    second_got = swap_dp(second_sent)
    kept_grad, sent = halves(preact_grad_all)
    first_sent = dot(tokens_all, sent, 0, 0)
    second_kept = dot(hidden_all, kept, 0, 0)
    parts = line_terms(out_terms, from_down, from_up)
    up, down, first_sent, second_kept, *parts = gate(
        *near_terms(in_terms, low, high), first_sent, second_kept, *parts
    )
    low, high = both(up, down, shift_y)
    first_got = swap_dp(first_sent)
    second_sum = (second_kept + second_got).astype(bf16)
    first_kept = dot(tokens_all, kept_grad, 0, 0)
    *in_parts, first_kept = gate(*line_terms(in_terms, low, high), first_kept)
    right, far, left = send_straight(in_parts[1:], shift_x)
    input_grad = in_parts[0] + right + far + left
    right, far, left = send_straight(parts[1:], shift_y)
    output = parts[0] + right + far + left
    first_sum = (first_kept + first_got).astype(bf16)
    return output.astype(bf16), input_grad.astype(bf16), first_sum, second_sum


def solution(mesh):
    in_specs = (P(("col", "dp"), "row"), P("row", "col"), P("col", "row"), P(("col", "dp"), "row"))
    out_specs = (
        P(("col", "dp"), "row"),
        P(("col", "dp"), "row"),
        P("row", ("col", "dp")),
        P("col", ("row", "dp")),
    )
    return jax.shard_map(shards, mesh=mesh, in_specs=in_specs, out_specs=out_specs, check_vma=False)
```

```python
import jax
import jax.numpy as jnp
from jax import lax
from jax.experimental import pallas as pl
from jax.experimental.pallas import tpu as pltpu
from jax.sharding import PartitionSpec as P

root_half = 0.7071067811865476
inv_root_tau = 0.3989422804014327
f32, bf16 = jnp.float32, jnp.bfloat16


def gelu_value(value):
    return value * 0.5 * (1.0 + lax.erf(value * root_half))


def gelu_slope(value):
    normal_cdf = 0.5 * (1.0 + lax.erf(value * root_half))
    return normal_cdf + value * jnp.exp(-0.5 * value * value) * inv_root_tau


def dot(left, right, left_dim=1, right_dim=0):
    return lax.dot_general(
        left, right, (((left_dim,), (right_dim,)), ((), ())), preferred_element_type=f32
    )


def shift_z(value, step):
    return lax.ppermute(value, "row", [(i, (i + step) % 8) for i in range(8)])


def shift_x(value, step):
    pairs = [(y * 4 + x, y * 4 + (x + step) % 4) for y in range(4) for x in range(4)]
    return lax.ppermute(value, "col", pairs)


def shift_y(value, step):
    pairs = [(y * 4 + x, (y + step) % 4 * 4 + x) for y in range(4) for x in range(4)]
    return lax.ppermute(value, "col", pairs)


def swap_dp(value):
    return lax.ppermute(value, "dp", [(0, 1), (1, 0)])


def gate(*arrays, after=()):
    def kernel(*refs):
        pass

    return pl.pallas_call(
        kernel,
        out_shape=[jax.ShapeDtypeStruct(array.shape, array.dtype) for array in arrays],
        in_specs=[pl.BlockSpec(memory_space=pl.ANY)] * (len(arrays) + len(after)),
        out_specs=[pl.BlockSpec(memory_space=pl.ANY)] * len(arrays),
        input_output_aliases={i: i for i in range(len(arrays))},
        compiler_params=pltpu.CompilerParams(vmem_limit_bytes=2**18),
        name="gate",
    )(*arrays, *after)


def lay(groups, place=None, after=()):
    shift = jnp.zeros((1,), jnp.int32) if place is None else place.astype(jnp.int32).reshape(1)
    arrays = [part for parts, _ in groups for _, part in parts]
    rows = [sum(part.shape[0] for _, part in parts) for parts, _ in groups]
    width = arrays[0].shape[1]

    def kernel(shift_ref, *refs):
        sources, outs, sems = refs[: len(arrays)], refs[-1 - len(groups) : -1], refs[-1]
        copies = []
        at = 0
        for (parts, spread), out in zip(groups, outs):
            for first, part in parts:
                if place is not None:
                    first = lax.rem(shift_ref[0] * 128 + first, out.shape[0])
                    first = pl.multiple_of(first, 64)
                size = part.shape[0] if spread == 64 else 64
                for row in range(0, part.shape[0], size):
                    target = out.at[pl.ds(first + row // 64 * spread, size)]
                    source = sources[at].at[pl.ds(row, size)]
                    copies.append(pltpu.make_async_copy(source, target, sems.at[len(copies)]))
                at += 1
        for copy in copies:
            copy.start()
        for copy in copies:
            copy.wait()

    size = sum(rows) * width * arrays[0].dtype.itemsize
    return pl.pallas_call(
        kernel,
        out_shape=[jax.ShapeDtypeStruct((count, width), arrays[0].dtype) for count in rows],
        in_specs=[pl.BlockSpec(memory_space=pltpu.SMEM)]
        + [pl.BlockSpec(memory_space=pl.ANY)] * (len(arrays) + len(after)),
        out_specs=[pl.BlockSpec(memory_space=pltpu.VMEM)] * len(groups),
        scratch_shapes=[pltpu.SemaphoreType.DMA((sum(rows) // 64,))],
        cost_estimate=pl.CostEstimate(flops=0, bytes_accessed=2 * size, transcendentals=0),
        compiler_params=pltpu.CompilerParams(vmem_limit_bytes=size + 2**20),
        name="lay",
    )(shift, *arrays, *after)


def send_line(block):
    return [(0, block), (64, shift_x(block, -1)), (128, shift_x(block, 2)), (192, shift_x(block, 1))]


def lay_plane(line, up, down, across):
    return lay([([(0, line), (256, up), (512, across[0]), (640, across[1]), (768, down)], 64)])[0]


def by_owner(value, col):
    def kernel(col_ref, source, out, sems):
        y, x = lax.div(col_ref[0], 4), lax.rem(col_ref[0], 4)
        copies = []
        for i in range(16):
            owner = lax.rem(y + i // 4, 4) * 4 + lax.rem(x + i % 4, 4)
            target = out.at[pl.ds(pl.multiple_of(owner * 64, 64), 64)]
            copies.append(pltpu.make_async_copy(source.at[pl.ds(i * 64, 64)], target, sems.at[i]))
        for copy in copies:
            copy.start()
        for copy in copies:
            copy.wait()

    size = value.size * value.dtype.itemsize
    return pl.pallas_call(
        kernel,
        out_shape=jax.ShapeDtypeStruct(value.shape, value.dtype),
        in_specs=[pl.BlockSpec(memory_space=pltpu.SMEM), pl.BlockSpec(memory_space=pl.ANY)],
        out_specs=pl.BlockSpec(memory_space=pltpu.VMEM),
        scratch_shapes=[pltpu.SemaphoreType.DMA((16,))],
        cost_estimate=pl.CostEstimate(flops=0, bytes_accessed=2 * size, transcendentals=0),
        compiler_params=pltpu.CompilerParams(vmem_limit_bytes=size + 2**20),
        name="by_owner",
    )(col.astype(jnp.int32).reshape(1), value)


def ring_terms(partial, first):
    width = partial.shape[1]
    if first is shift_x:
        return [partial.reshape(4, 4, 64, width)[:, i].reshape(256, width) for i in range(4)]
    return [partial[256 * i : 256 * i + 256] for i in range(4)]


def far_terms(terms):
    half = terms[2].shape[1] // 2
    return terms[2][:, :half], terms[2][:, half:]


def near_terms(terms, from_down, from_up):
    half = terms[2].shape[1] // 2
    up = jnp.concatenate([terms[1][:, :half] + from_down, terms[1][:, half:]], axis=1)
    down = jnp.concatenate([terms[3][:, :half], terms[3][:, half:] + from_up], axis=1)
    return up.astype(bf16), down.astype(bf16)


def line_terms(terms, from_down, from_up):
    line = terms[0] + from_down.astype(f32) + from_up.astype(f32)
    return [line[64 * i : 64 * i + 64] for i in range(4)]


def send_straight(parts, way):
    return way(parts[0], 1), way(parts[1], 2), way(parts[2], -1)


def both(ahead, behind, way=shift_z):
    return way(ahead, 1), way(behind, -1)


def shards(tokens, in_weight, out_weight, output_grad):
    z, dp = lax.axis_index("row"), lax.axis_index("dp")

    def halves(value):
        width = value.shape[1] // 2
        left, right = value[:, :width], value[:, width:]
        return jnp.where(dp == 0, left, right), jnp.where(dp == 0, right, left)

    def term(value, weight, weight_dim):
        def of(k):
            block = lax.dynamic_slice_in_dim(value, (z + k) % 8 * 128, 128, axis=0)
            return dot(block, weight, 1, weight_dim)

        return of

    def far_of(of):
        far = of(4).astype(bf16)
        return far[:, :768], far[:, 768:]

    def next_of(of, k, ahead, behind):
        if k == 3:
            three, five = of(3), of(5)
            ahead = jnp.concatenate([three[:, :768] + ahead.astype(f32), three[:, 768:]], axis=1)
            behind = jnp.concatenate([five[:, :768], five[:, 768:] + behind.astype(f32)], axis=1)
        else:
            ahead, behind = of(k) + ahead.astype(f32), of(8 - k) + behind.astype(f32)
        return ahead.astype(bf16), behind.astype(bf16)

    (line,) = lay([(send_line(tokens), 64)])
    (late,) = gate(output_grad, after=[line])
    up, down = shift_y(line, -1), shift_y(line, 1)
    found = send_line(late)
    across = shift_y(up[:128], -1), shift_y(down[128:], 1)
    (grad_line,) = lay([(found, 64)])
    grad_up, grad_down = shift_y(grad_line, -1), shift_y(grad_line, 1)
    tokens_all = lay_plane(line, up, down, across)
    across = shift_y(grad_up[:128], -1), shift_y(grad_down[128:], 1)
    grad_all = lay_plane(grad_line, grad_up, grad_down, across)
    preact_of, grad_of = term(tokens_all, in_weight, 0), term(grad_all, out_weight, 1)

    ahead, behind = both(*far_of(preact_of))
    ahead, behind = both(*next_of(preact_of, 3, ahead, behind))
    low, high = gate(*far_of(grad_of), after=[ahead, behind])
    ahead, behind = both(*next_of(preact_of, 2, ahead, behind))
    low, high = both(low, high)
    low, high = gate(*next_of(grad_of, 3, low, high), after=[ahead, behind])
    ahead, behind = both(*next_of(preact_of, 1, ahead, behind))
    low, high = both(low, high)
    preact = preact_of(0) + ahead.astype(f32) + behind.astype(f32)
    hidden = gelu_value(preact).astype(bf16)
    slope = gelu_slope(preact)
    low, high = gate(*next_of(grad_of, 2, low, high), after=[hidden])
    found = [(0, hidden)]
    ahead, behind = both(hidden, hidden)
    found += [(896, ahead), (128, behind)]
    low, high = both(low, high)
    low, high = gate(*next_of(grad_of, 1, low, high), after=[ahead, behind])
    ahead, behind = both(ahead, behind)
    found += [(768, ahead), (256, behind)]
    low, high = both(low, high)
    hidden_grad = grad_of(0) + low.astype(f32) + high.astype(f32)
    (preact_grad,) = gate((hidden_grad * slope).astype(bf16), after=[ahead, behind])
    ahead, behind = both(ahead, behind)
    found += [(640, ahead), (384, behind)]
    found_grad = [(0, preact_grad)]
    low, high = both(preact_grad, preact_grad)
    low, high = gate(low, high, after=[ahead, behind])
    found_grad += [(896, low), (128, high)]
    ahead, behind = both(ahead[64:], behind[:64])
    found += [(576, ahead), (512, behind)]
    low, high = both(low, high)
    low, high = gate(low, high, after=[ahead, behind])
    found_grad += [(768, low), (256, high)]
    low, high = both(low, high)
    (hidden_all,) = lay([(found, 64)], z)
    output = by_owner(dot(hidden_all, out_weight).astype(bf16), lax.axis_index("col"))
    low, high = gate(low, high, after=[output])
    found_grad += [(640, low), (384, high)]
    output = lax.all_to_all(output, "col", 0, 0, tiled=True).reshape(16, 64, -1)
    low, high = both(low[64:], high[:64])
    found_grad += [(576, low), (512, high)]
    kept, sent = halves(grad_all)
    second_sent = dot(hidden_all, sent, 0, 0)
    second_sum = (dot(hidden_all, kept, 0, 0) + swap_dp(second_sent)).astype(bf16)

    (preact_grad_all,) = lay([(found_grad, 64)], z)
    in_terms = ring_terms(dot(preact_grad_all, in_weight, 1, 1), shift_y)
    far, far_up, preact_grad_all = gate(*far_terms(in_terms), preact_grad_all)
    low, high = shift_y(far, 1), shift_y(far_up, -1)
    kept, sent = halves(preact_grad_all)
    first_sent = dot(tokens_all, sent, 0, 0)
    up, down, first_sent, kept = gate(*near_terms(in_terms, low, high), first_sent, kept)
    low, high = shift_y(up, 1), shift_y(down, -1)
    first_sum = (dot(tokens_all, kept, 0, 0) + swap_dp(first_sent)).astype(bf16)
    output = output.astype(f32).sum(0).astype(bf16)
    parts = gate(*line_terms(in_terms, low, high), after=[output])
    right, far, left = send_straight(parts[1:], shift_x)
    (right,) = gate(right, after=[first_sum, second_sum])
    input_grad = (parts[0] + right + far + left).astype(bf16)
    return output, input_grad, first_sum, second_sum


def solution(mesh):
    in_specs = (P(("col", "dp"), "row"), P("row", "col"), P("col", "row"), P(("col", "dp"), "row"))
    out_specs = (
        P(("col", "dp"), "row"),
        P(("col", "dp"), "row"),
        P("row", ("col", "dp")),
        P("col", ("row", "dp")),
    )
    return jax.shard_map(shards, mesh=mesh, in_specs=in_specs, out_specs=out_specs, check_vma=False)
```

```python
import jax
import jax.numpy as jnp
from jax import lax
from jax.experimental import pallas as pl
from jax.experimental.pallas import tpu as pltpu
from jax.sharding import PartitionSpec as P

root_half = 0.7071067811865476
inv_root_tau = 0.3989422804014327
f32, bf16 = jnp.float32, jnp.bfloat16


def gelu_value(value):
    return value * 0.5 * (1.0 + lax.erf(value * root_half))


def gelu_slope(value):
    normal_cdf = 0.5 * (1.0 + lax.erf(value * root_half))
    return normal_cdf + value * jnp.exp(-0.5 * value * value) * inv_root_tau


def dot(left, right, left_dim=1, right_dim=0):
    return lax.dot_general(
        left, right, (((left_dim,), (right_dim,)), ((), ())), preferred_element_type=f32
    )


def shift_z(value, step):
    return lax.ppermute(value, "row", [(i, (i + step) % 8) for i in range(8)])


def shift_x(value, step):
    pairs = [(y * 4 + x, y * 4 + (x + step) % 4) for y in range(4) for x in range(4)]
    return lax.ppermute(value, "col", pairs)


def shift_y(value, step):
    pairs = [(y * 4 + x, (y + step) % 4 * 4 + x) for y in range(4) for x in range(4)]
    return lax.ppermute(value, "col", pairs)


def swap_dp(value):
    return lax.ppermute(value, "dp", [(0, 1), (1, 0)])


def gate(*arrays, after=()):
    def kernel(*refs):
        pass

    return pl.pallas_call(
        kernel,
        out_shape=[jax.ShapeDtypeStruct(array.shape, array.dtype) for array in arrays],
        in_specs=[pl.BlockSpec(memory_space=pl.ANY)] * (len(arrays) + len(after)),
        out_specs=[pl.BlockSpec(memory_space=pl.ANY)] * len(arrays),
        input_output_aliases={i: i for i in range(len(arrays))},
        compiler_params=pltpu.CompilerParams(vmem_limit_bytes=2**18),
        name="gate",
    )(*arrays, *after)


def lay(groups, place=None, after=()):
    shift = jnp.zeros((1,), jnp.int32) if place is None else place.astype(jnp.int32).reshape(1)
    arrays = [part for parts, _ in groups for _, part in parts]
    rows = [sum(part.shape[0] for _, part in parts) for parts, _ in groups]
    width = arrays[0].shape[1]

    def kernel(shift_ref, *refs):
        sources, outs, sems = refs[: len(arrays)], refs[-1 - len(groups) : -1], refs[-1]
        copies = []
        at = 0
        for (parts, spread), out in zip(groups, outs):
            for first, part in parts:
                if place is not None:
                    first = lax.rem(shift_ref[0] * 128 + first, out.shape[0])
                    first = pl.multiple_of(first, 64)
                size = part.shape[0] if spread == 64 else 64
                for row in range(0, part.shape[0], size):
                    target = out.at[pl.ds(first + row // 64 * spread, size)]
                    source = sources[at].at[pl.ds(row, size)]
                    copies.append(pltpu.make_async_copy(source, target, sems.at[len(copies)]))
                at += 1
        for copy in copies:
            copy.start()
        for copy in copies:
            copy.wait()

    size = sum(rows) * width * arrays[0].dtype.itemsize
    return pl.pallas_call(
        kernel,
        out_shape=[jax.ShapeDtypeStruct((count, width), arrays[0].dtype) for count in rows],
        in_specs=[pl.BlockSpec(memory_space=pltpu.SMEM)]
        + [pl.BlockSpec(memory_space=pl.ANY)] * (len(arrays) + len(after)),
        out_specs=[pl.BlockSpec(memory_space=pltpu.VMEM)] * len(groups),
        scratch_shapes=[pltpu.SemaphoreType.DMA((sum(rows) // 64,))],
        cost_estimate=pl.CostEstimate(flops=0, bytes_accessed=2 * size, transcendentals=0),
        compiler_params=pltpu.CompilerParams(vmem_limit_bytes=size + 2**20),
        name="lay",
    )(shift, *arrays, *after)


def send_line(block):
    return [(0, block), (64, shift_x(block, -1)), (128, shift_x(block, 2)), (192, shift_x(block, 1))]


def lay_plane(line, up, down, across):
    return lay([([(0, line), (256, up), (512, across[0]), (640, across[1]), (768, down)], 64)])[0]


def by_owner(value, col):
    def kernel(col_ref, source, out, sems):
        y, x = lax.div(col_ref[0], 4), lax.rem(col_ref[0], 4)
        copies = []
        for i in range(16):
            owner = lax.rem(y + i // 4, 4) * 4 + lax.rem(x + i % 4, 4)
            target = out.at[pl.ds(pl.multiple_of(owner * 64, 64), 64)]
            copies.append(pltpu.make_async_copy(source.at[pl.ds(i * 64, 64)], target, sems.at[i]))
        for copy in copies:
            copy.start()
        for copy in copies:
            copy.wait()

    size = value.size * value.dtype.itemsize
    return pl.pallas_call(
        kernel,
        out_shape=jax.ShapeDtypeStruct(value.shape, value.dtype),
        in_specs=[pl.BlockSpec(memory_space=pltpu.SMEM), pl.BlockSpec(memory_space=pl.ANY)],
        out_specs=pl.BlockSpec(memory_space=pltpu.VMEM),
        scratch_shapes=[pltpu.SemaphoreType.DMA((16,))],
        cost_estimate=pl.CostEstimate(flops=0, bytes_accessed=2 * size, transcendentals=0),
        compiler_params=pltpu.CompilerParams(vmem_limit_bytes=size + 2**20),
        name="by_owner",
    )(col.astype(jnp.int32).reshape(1), value)


def ring_terms(partial, first):
    width = partial.shape[1]
    if first is shift_x:
        return [partial.reshape(4, 4, 64, width)[:, i].reshape(256, width) for i in range(4)]
    return [partial[256 * i : 256 * i + 256] for i in range(4)]


def far_terms(terms):
    half = terms[2].shape[1] // 2
    return terms[2][:, :half], terms[2][:, half:]


def near_terms(terms, from_down, from_up):
    half = terms[2].shape[1] // 2
    up = jnp.concatenate([terms[1][:, :half] + from_down, terms[1][:, half:]], axis=1)
    down = jnp.concatenate([terms[3][:, :half], terms[3][:, half:] + from_up], axis=1)
    return up.astype(bf16), down.astype(bf16)


def line_terms(terms, from_down, from_up):
    line = terms[0] + from_down.astype(f32) + from_up.astype(f32)
    return [line[64 * i : 64 * i + 64] for i in range(4)]


def send_straight(parts, way):
    return way(parts[0], 1), way(parts[1], 2), way(parts[2], -1)


def both(ahead, behind, way=shift_z):
    return way(ahead, 1), way(behind, -1)


def shards(tokens, in_weight, out_weight, output_grad):
    z, dp = lax.axis_index("row"), lax.axis_index("dp")

    def halves(value):
        width = value.shape[1] // 2
        left, right = value[:, :width], value[:, width:]
        return jnp.where(dp == 0, left, right), jnp.where(dp == 0, right, left)

    def term(value, weight, weight_dim):
        def of(k):
            block = lax.dynamic_slice_in_dim(value, (z + k) % 8 * 128, 128, axis=0)
            return dot(block, weight, 1, weight_dim)

        return of

    def far_of(of):
        far = of(4).astype(bf16)
        return far[:, :768], far[:, 768:]

    def next_of(of, k, ahead, behind):
        if k == 3:
            three, five = of(3), of(5)
            ahead = jnp.concatenate([three[:, :768] + ahead.astype(f32), three[:, 768:]], axis=1)
            behind = jnp.concatenate([five[:, :768], five[:, 768:] + behind.astype(f32)], axis=1)
        else:
            ahead, behind = of(k) + ahead.astype(f32), of(8 - k) + behind.astype(f32)
        return ahead.astype(bf16), behind.astype(bf16)

    (line,) = lay([(send_line(tokens), 64)])
    (late,) = lay([([(0, output_grad)], 64)], after=[line])
    up, down = shift_y(line, -1), shift_y(line, 1)
    found = send_line(late)
    across = shift_y(up[:128], -1), shift_y(down[128:], 1)
    (grad_line,) = lay([(found, 64)])
    grad_up, grad_down = shift_y(grad_line, -1), shift_y(grad_line, 1)
    tokens_all = lay_plane(line, up, down, across)
    across = shift_y(grad_up[:128], -1), shift_y(grad_down[128:], 1)
    grad_all = lay_plane(grad_line, grad_up, grad_down, across)
    preact_of, grad_of = term(tokens_all, in_weight, 0), term(grad_all, out_weight, 1)

    ahead, behind = both(*far_of(preact_of))
    ahead, behind = both(*next_of(preact_of, 3, ahead, behind))
    low, high = gate(*far_of(grad_of), after=[ahead, behind])
    ahead, behind = both(*next_of(preact_of, 2, ahead, behind))
    low, high = both(low, high)
    low, high = gate(*next_of(grad_of, 3, low, high), after=[ahead, behind])
    ahead, behind = both(*next_of(preact_of, 1, ahead, behind))
    low, high = both(low, high)
    preact = preact_of(0) + ahead.astype(f32) + behind.astype(f32)
    hidden = gelu_value(preact).astype(bf16)
    slope = gelu_slope(preact)
    low, high = gate(*next_of(grad_of, 2, low, high), after=[hidden])
    found = [(0, hidden)]
    ahead, behind = both(hidden, hidden)
    found += [(896, ahead), (128, behind)]
    low, high = both(low, high)
    low, high = gate(*next_of(grad_of, 1, low, high), after=[ahead, behind])
    ahead, behind = both(ahead, behind)
    found += [(768, ahead), (256, behind)]
    low, high = both(low, high)
    hidden_grad = grad_of(0) + low.astype(f32) + high.astype(f32)
    (preact_grad,) = gate((hidden_grad * slope).astype(bf16), after=[ahead, behind])
    ahead, behind = both(ahead, behind)
    found += [(640, ahead), (384, behind)]
    found_grad = [(0, preact_grad)]
    low, high = both(preact_grad, preact_grad)
    low, high = gate(low, high, after=[ahead, behind])
    found_grad += [(896, low), (128, high)]
    ahead, behind = both(ahead[64:], behind[:64])
    found += [(576, ahead), (512, behind)]
    low, high = both(low, high)
    low, high = gate(low, high, after=[ahead, behind])
    found_grad += [(768, low), (256, high)]
    low, high = both(low, high)
    (hidden_all,) = lay([(found, 64)], z)
    output = by_owner(dot(hidden_all, out_weight).astype(bf16), lax.axis_index("col"))
    low, high = gate(low, high, after=[output])
    found_grad += [(640, low), (384, high)]
    output = lax.all_to_all(output, "col", 0, 0, tiled=True).reshape(16, 64, -1)
    low, high = both(low[64:], high[:64])
    found_grad += [(576, low), (512, high)]
    kept, sent = halves(grad_all)
    second_sent = dot(hidden_all, sent, 0, 0)
    second_sum = (dot(hidden_all, kept, 0, 0) + swap_dp(second_sent)).astype(bf16)

    (preact_grad_all,) = lay([(found_grad, 64)], z)
    in_terms = ring_terms(dot(preact_grad_all, in_weight, 1, 1), shift_y)
    far, far_up, preact_grad_all = gate(*far_terms(in_terms), preact_grad_all)
    low, high = shift_y(far, 1), shift_y(far_up, -1)
    kept, sent = halves(preact_grad_all)
    first_sent = dot(tokens_all, sent, 0, 0)
    up, down, first_sent = gate(*near_terms(in_terms, low, high), first_sent)
    low, high = shift_y(up, 1), shift_y(down, -1)
    first_sum = (dot(tokens_all, kept, 0, 0) + swap_dp(first_sent)).astype(bf16)
    output = output.astype(f32).sum(0).astype(bf16)
    parts = gate(*line_terms(in_terms, low, high), after=[output])
    right, far, left = send_straight(parts[1:], shift_x)
    (right,) = gate(right, after=[first_sum, second_sum])
    input_grad = (parts[0] + right + far + left).astype(bf16)
    return output, input_grad, first_sum, second_sum


def solution(mesh):
    in_specs = (P(("col", "dp"), "row"), P("row", "col"), P("col", "row"), P(("col", "dp"), "row"))
    out_specs = (
        P(("col", "dp"), "row"),
        P(("col", "dp"), "row"),
        P("row", ("col", "dp")),
        P("col", ("row", "dp")),
    )
    return jax.shard_map(shards, mesh=mesh, in_specs=in_specs, out_specs=out_specs, check_vma=False)
```
